32 devices in a mesh: ga: 2 (over x), gx: 8 (over z, y), yz: 2 (over core).
Axes of the slice: x: 2, y: 2, z: 4, core: 2. Of those that a mesh axis runs over, the one named last changes fastest.
Arguments:
- tokens: bfloat16 [2, 64, 18432], P(None, ('ga', 'gx'), 'yz'), parts along dimension 1, may hold values from -6 to 6
- norm_gain: bfloat16 [18432], P('yz'), may hold values from 0.099609375 to 1.8984375
- query_weight: bfloat16 [18432, 8192], P('yz', 'gx'), may hold values from -0.046875 to 0.046875
- kv_weight: bfloat16 [18432, 512], P('yz', 'gx'), may hold values from -0.046875 to 0.046875
- out_weight: bfloat16 [8192, 18432], P('gx', 'yz'), may hold values from -0.0625 to 0.0625
- cache: bfloat16 [64, 1024, 512], P(('ga', 'gx', 'yz')), parts along dimension 0, may hold values from -300 to 300
- cache_lengths: int32 [64], P(('ga', 'gx', 'yz')), parts along dimension 0, may hold values from 1 to 1024, as said below
Outputs:
- updated: bfloat16 [2, 64, 18432], P(None, ('ga', 'gx'), 'yz'), parts along dimension 1
The draws below stay inside these ranges and needn't reach their ends.
There are 2 independent parts, one for each index of `ga`. The reference program is written for one: setup_inputs(seed, part) draws one part's arguments, and reference() takes and returns one part's arrays. A program takes and returns all parts, laid end to end along the dimension named above; an argument that names none is the same for every part. Nothing has to cross between parts.
Inputs may be any that keep to these rules, and one draw needn't show every extreme that they name: `cache_lengths`: some sequence has all 1024 slots filled.
All inputs are finite; a program needn't handle non-finite values.
Results may differ from the reference program's by a relative error of at most 0.0059.
Values may be sent and summed in bfloat16 or wider, within the bound.
A program may use at most 128 MiB of HBM per device.

```python
import jax
import jax.numpy as jnp
from jax import lax

D = 18432
HEADS = 32
DH = 256
CACHE = 1024
STEPS = 2
BATCH = 32


def draw_cache(key, part):
    key = jax.random.fold_in(key, 11)
    key_one, key_two = jax.random.split(key, 2)
    stored_keys = jnp.clip(jax.random.normal(key_one, (BATCH, CACHE, DH), jnp.float32), -6.0, 6.0)
    stored_values = 4.0 * jnp.clip(jax.random.normal(key_two, (BATCH, CACHE, DH), jnp.float32), -6.0, 6.0)
    return jnp.concatenate([stored_keys, stored_values], -1).astype(jnp.bfloat16)


def draw_cache_lengths(key, part):
    key = jax.random.fold_in(key, 23)
    key_one, key_two = jax.random.split(key)
    lengths = jax.random.randint(key_one, (BATCH,), 1, CACHE + 1)
    chosen = jax.random.randint(key_two, (), 0, BATCH)
    return jnp.where(jnp.arange(BATCH) == chosen, CACHE, lengths).astype(jnp.int32)


def level_of(key, shape, pieces, smallest, top_value):
    factor_of, own = 1.0, jax.random.fold_in(key, 6)
    for axis_at, blocks in pieces:
        steps = jnp.exp(jax.random.uniform(jax.random.fold_in(own, axis_at), (blocks,), jnp.float32, smallest / len(pieces), top_value / len(pieces)))
        factor_of = factor_of * jnp.repeat(steps, shape[axis_at] // blocks).reshape([-1 if axis == axis_at else 1 for axis in range(len(shape))])
    return factor_of


def noise(own_key, shape, scale, bound, pieces=(), kind=jnp.bfloat16):
    result = scale * jax.random.normal(own_key, shape, jnp.float32)
    if pieces:
        result = result * level_of(own_key, shape, pieces, -0.22, 0.18)
    return jnp.clip(result, -bound, bound).astype(kind)


def setup_inputs(seed: int = 0, part: int = 0) -> dict:
    seeds = jax.random.split(jax.random.key(seed), 8)
    part_splits = jax.random.split(jax.random.fold_in(seeds[7], part), 8)
    tokens = noise(part_splits[0], (STEPS, BATCH, D), 1.0, 6.0, ((1, 8), (2, 2)))
    norm_gain = jnp.clip(1.0 + 0.18 * jax.random.normal(seeds[1], (D,), jnp.float32), 0.099609375, 1.8984375).astype(jnp.bfloat16)
    query_weight = noise(seeds[2], (D, HEADS * DH), D ** -0.5, 0.046875, ((0, 2), (1, 8)))
    kv_weight = noise(seeds[3], (D, 2 * DH), D ** -0.5, 0.046875, ((0, 2), (1, 8)))
    out_weight = noise(seeds[4], (HEADS * DH, D), (HEADS * DH) ** -0.5, 0.0625, ((0, 8), (1, 2)))
    cache = draw_cache(jax.random.fold_in(jax.random.fold_in(seeds[7], part), 71), part)
    cache_lengths = draw_cache_lengths(jax.random.fold_in(jax.random.fold_in(seeds[7], part), 71), part)
    return dict(tokens=tokens, norm_gain=norm_gain, query_weight=query_weight, kv_weight=kv_weight, out_weight=out_weight, cache=cache, cache_lengths=cache_lengths)


def layer_norm(values, norm_gain):
    widened = values.astype(jnp.float32)
    average = lax.optimization_barrier(jnp.sum(widened, -1, keepdims=True)) / D
    second = lax.optimization_barrier(jnp.sum(widened * widened, -1, keepdims=True)) / D
    spread = second - average * average
    scaled = (widened - average) * lax.rsqrt(spread + 1e-05) * norm_gain.astype(jnp.float32)
    return scaled.astype(jnp.bfloat16)

def reference(tokens, norm_gain, query_weight, kv_weight, out_weight, cache, cache_lengths):
    normed = layer_norm(tokens.reshape(STEPS * BATCH, D), norm_gain)
    queries = jnp.dot(normed, query_weight, preferred_element_type=jnp.float32).astype(jnp.bfloat16)
    queries = queries.reshape(STEPS, BATCH, HEADS, DH)
    new_kv = jnp.dot(normed, kv_weight, preferred_element_type=jnp.float32).astype(jnp.bfloat16)
    new_kv = new_kv.reshape(STEPS, BATCH, 2 * DH)
    cache_keys = cache[:, :, :DH].astype(jnp.float32)
    cache_values = cache[:, :, DH:].astype(jnp.float32)
    filled = jnp.arange(CACHE, dtype=jnp.int32)[None, :] < cache_lengths[:, None]
    factor = DH ** (-0.5)
    results = []
    for step in range(STEPS):
        query = queries[step].astype(jnp.float32)
        old_scores = jnp.einsum('bhd,bcd->bhc', query, cache_keys) * factor
        old_scores = jnp.where(filled[:, None, :], old_scores, -jnp.inf)
        fresh_keys = new_kv[:step + 1, :, :DH].astype(jnp.float32)
        fresh_values = new_kv[:step + 1, :, DH:].astype(jnp.float32)
        new_scores = jnp.einsum('bhd,sbd->bhs', query, fresh_keys) * factor
        scores = jnp.concatenate([old_scores, new_scores], -1)
        highest = lax.optimization_barrier(jnp.max(scores, -1, keepdims=True))
        raised = jnp.exp(scores - highest)
        weights = (raised / lax.optimization_barrier(jnp.sum(raised, -1, keepdims=True))).astype(jnp.bfloat16)
        weighted = jnp.einsum('bhc,bcd->bhd', weights[..., :CACHE].astype(jnp.float32), cache_values)
        weighted = weighted + jnp.einsum('bhs,sbd->bhd', weights[..., CACHE:].astype(jnp.float32), fresh_values)
        attended = weighted.astype(jnp.bfloat16).reshape(BATCH, HEADS * DH)
        mixed = tokens[step].astype(jnp.float32) + jnp.dot(attended, out_weight, preferred_element_type=jnp.float32)
        results.append(mixed.astype(jnp.bfloat16))
    return jnp.stack(results)
```

```python
import functools

import jax
import jax.numpy as jnp
from jax import lax
from jax.experimental import pallas as pl
from jax.experimental.pallas import tpu as pltpu
from jax.sharding import PartitionSpec as P

BF = jnp.bfloat16
F32 = jnp.float32
TAIL = 128
PAIR = 2
LANES = 128


def up(n, m):
    return -(-n // m) * m


def iotas(shape):
    return lax.broadcasted_iota(jnp.int32, shape, 0), lax.broadcasted_iota(jnp.int32, shape, 1)


def pick(rows, cols, source):
    o, i = iotas((rows, cols))
    return jnp.where(source(o) == i, 1.0, 0.0).astype(BF)


def mm(a, b):
    return jnp.dot(a, b, preferred_element_type=F32)


def kernel(
    dims,
    lens, tok, gain, wq_h, wkv_h, wo_h, cache_h,
    out,
    wq, wkv, wo, ext, x32, st, st_r, xg, xall, acc, acc_r,
    qs, qr, kvs, kvr, ats, atr, att, own, ys, yr, zs, zr,
    w_sem, st_sem, ag_s, fw_s, ag_r, ac_sem, q_s, q_r, kv_s, kv_r, at_s, at_r, y_s, y_r, z_s, z_r,
):
    G, C, S, R, F, NB, HL, DH, KVC, CACHE, NC, QB = dims
    T = S * R
    Z = G // PAIR
    H = G * HL
    M = G * T
    fc = F // NC
    half = fc // 2
    W = S * NB
    QW = HL * DH
    g = lax.axis_index("gx")
    c = lax.axis_index("yz")
    z = g // PAIR
    y = g % PAIR
    yp = z * PAIR + (1 - y)

    for k in range(NC):
        rows = pl.ds(k * fc, fc)
        pltpu.make_async_copy(wq_h.at[rows], wq.at[rows], w_sem.at[k]).start()
    pltpu.make_async_copy(wkv_h, wkv, w_sem.at[NC]).start()
    for b in range(NB):
        pltpu.make_async_copy(cache_h.at[b], ext.at[b, pl.ds(0, CACHE)], w_sem.at[NC + 1 + b]).start()
    pltpu.make_async_copy(wo_h, wo, w_sem.at[NC + 1 + NB]).start()

    bar = pltpu.get_barrier_semaphore()
    n_dev = G * C
    me = g * C + c

    def greet(t, _):
        o = (me + t) % n_dev
        pl.semaphore_signal(bar, inc=1, device_id={"gx": o // C, "yz": o % C}, device_id_type=pl.DeviceIdType.MESH)
        return 0

    lax.fori_loop(1, n_dev, greet, 0)

    for s in range(S):
        x32[pl.ds(s * R, R), :] = tok[s].astype(F32)
    x = x32[...]
    st[0] = jnp.broadcast_to(jnp.sum(x, -1, keepdims=True), (T, LANES))
    st[1] = jnp.broadcast_to(jnp.sum(x * x, -1, keepdims=True), (T, LANES))
    pl.semaphore_wait(bar, n_dev - 1)

    def rcopy(src, dst, ss, rs, dev):
        return pltpu.make_async_remote_copy(
            src_ref=src, dst_ref=dst, send_sem=ss, recv_sem=rs, device_id=dev, device_id_type=pl.DeviceIdType.MESH
        )

    st_copy = rcopy(st, st_r, st_sem.at[0], st_sem.at[1], {"yz": 1 - c})
    st_copy.start()
    for b in range(NB):
        ext[b, pl.ds(CACHE, TAIL), :] = jnp.zeros((TAIL, 2 * DH), BF)
    acc[...] = jnp.zeros_like(acc)
    st_copy.wait()
    D = F * C
    average = ((st[0] + st_r[0]) / D)[:, :1]
    spread = ((st[1] + st_r[1]) / D)[:, :1] - average * average
    inv = lax.rsqrt(spread + 1e-05)

    def ag(k, t):
        dev = yp if t == 0 else ((z + t) % Z) * PAIR + y
        return rcopy(xg.at[k, g], xg.at[k, g], ag_s.at[k, t], ag_r.at[k, g], {"gx": dev})

    def fw(k, t):
        o = ((z + t) % Z) * PAIR + y
        return rcopy(xg.at[k, o], xg.at[k, o], fw_s.at[k, t], ag_r.at[k, o], {"gx": yp})

    for k in range(NC):
        parts = []
        for p in range(2):
            cols = pl.ds(k * fc + p * half, half)
            parts.append((x32[:, cols] - average) * inv * gain[:, cols].astype(F32))
        xg[k, g] = jnp.concatenate(parts, 0).astype(BF)
        for t in range(1, Z):
            ag(k, t).start()
        ag(k, 0).start()

    for k in range(NC):
        for t in range(1, Z):
            o = ((z + t) % Z) * PAIR + y
            rcopy(xg.at[k, o], xg.at[k, o], fw_s.at[k, t], ag_r.at[k, o], {"gx": yp}).wait_recv()
            fw(k, t).start()

    for k in range(NC):
        for t in range(Z):
            o = ((z + t) % Z) * PAIR + (1 - y)
            rcopy(xg.at[k, o], xg.at[k, o], fw_s.at[k, t], ag_r.at[k, o], {"gx": yp}).wait_recv()
        rows = pl.ds(k * fc, fc)
        for p in range(2):
            block = xg[k].astype(F32)[:, p * T:(p + 1) * T, :].reshape(M, half)
            xall[:, pl.ds(k * fc + p * half, half)] = block.astype(BF)
        pltpu.make_async_copy(wq_h.at[rows], wq.at[rows], w_sem.at[k]).wait()
        if k == 0:
            pltpu.make_async_copy(wkv_h, wkv, w_sem.at[NC]).wait()

        def project(n, _):
            cols = pl.ds(pl.multiple_of(n * DH, DH), DH)
            acc[:, cols] += mm(xall[:, rows], wq[rows, cols])
            return 0

        lax.fori_loop(0, HL, project, 0)
        acc[:, pl.ds(QW, KVC)] += mm(xall[:, rows], wkv[rows, :])

    ac = rcopy(acc, acc_r, ac_sem.at[0], ac_sem.at[1], {"yz": 1 - c})
    ac.start()
    ac.wait()

    def from_w(o, width):
        return o // width, o % width

    def q_source(o):
        d, w = from_w(o, QB)
        hl, s, b = w // W, (w // NB) % S, w % NB
        return jnp.where(w < HL * W, hl * M + d * T + s * R + c * NB + b, -1)

    def kv_source(o):
        d, w = from_w(o, 16)
        return jnp.where(w < W, d * T + (w // NB) * R + c * NB + w % NB, -1)

    kv_all = (acc[:, pl.ds(QW, LANES)] + acc_r[:, pl.ds(QW, LANES)]).astype(BF)
    kvs[...] = mm(pick(G * 16, M, kv_source), kv_all).astype(BF).reshape(G, 16, LANES)
    q_all = jnp.concatenate(
        [(acc[:, pl.ds(n * DH, DH)] + acc_r[:, pl.ds(n * DH, DH)]).astype(BF) for n in range(HL)], 0
    )
    qs[...] = mm(pick(G * QB, HL * M, q_source), q_all).astype(BF).reshape(G, QB, DH)

    def q_copy(t):
        o = (g + t) % G
        return rcopy(qs.at[o], qr.at[g], q_s.at[t], q_r.at[g], {"gx": o})

    def kv_copy(t):
        o = (g + t) % G
        return rcopy(kvs.at[o], kvr.at[g], kv_s.at[t], kv_r.at[g], {"gx": o})

    def q_start(t, _):
        kv_copy(t).start()
        q_copy(t).start()
        return 0

    lax.fori_loop(1, G, q_start, 0)
    kvr[g] = kvs[g]
    qr[g] = qs[g]

    def q_wait(t, _):
        o = (g + t) % G
        rcopy(kvs.at[o], kvr.at[o], kv_s.at[t], kv_r.at[o], {"gx": o}).wait_recv()
        rcopy(qs.at[o], qr.at[o], q_s.at[t], q_r.at[o], {"gx": o}).wait_recv()
        return 0

    lax.fori_loop(1, G, q_wait, 0)

    fresh = jnp.zeros((16, 2 * DH), F32)
    for d in range(G):
        i, n = iotas((LANES, 2 * DH))
        spread_cols = jnp.where((i < KVC) & (n == i + d * KVC), 1.0, 0.0).astype(BF)
        fresh = fresh + mm(kvr[d], spread_cols)
    fresh = fresh.astype(BF)
    for b in range(NB):
        rows_b = mm(pick(16, 16, lambda o: jnp.where(o < S, o * NB + b, -1)), fresh)
        ext[b, pl.ds(CACHE, 16), :] = rows_b.astype(BF)

    HS = H * S

    def r_source(o):
        b, h, s = o // HS, (o // S) % H, o % S
        return (h // HL) * QB + (h % HL) * W + s * NB + b

    query = mm(pick(NB * HS, G * QB, r_source), qr[...].reshape(G * QB, DH)).astype(BF)
    slots = CACHE + TAIL
    factor = DH ** (-0.5)
    outs = []
    for b in range(NB):
        pltpu.make_async_copy(cache_h.at[b], ext.at[b, pl.ds(0, CACHE)], w_sem.at[NC + 1 + b]).wait()
        qb = query[b * HS:(b + 1) * HS]
        scores = lax.dot_general(
            qb, ext[b, :, pl.ds(0, DH)], (((1,), (1,)), ((), ())), preferred_element_type=F32
        ) * factor
        row, slot = iotas((HS, slots))
        seen = (slot < lens[b]) | ((slot >= CACHE) & (slot - CACHE <= row % S))
        scores = jnp.where(seen, scores, -jnp.inf)
        raised = jnp.exp(scores - jnp.max(scores, -1, keepdims=True))
        weights = (raised / jnp.sum(raised, -1, keepdims=True)).astype(BF)
        outs.append(mm(weights, ext[b, :, pl.ds(DH, DH)]).astype(BF))
    attended = jnp.concatenate(outs, 0)

    def a_source(o):
        d, w = from_w(o, QB)
        hl, s, b = w // W, (w // NB) % S, w % NB
        return jnp.where(w < HL * W, b * HS + (d * HL + hl) * S + s, -1)

    ats[...] = mm(pick(G * QB, NB * HS, a_source), attended).astype(BF).reshape(G, QB, DH)

    def at_copy(t):
        o = (me + t) % n_dev
        return rcopy(ats.at[o // C], atr.at[me], at_s.at[t], at_r.at[me], {"gx": o // C, "yz": o % C})

    def at_start(t, _):
        at_copy(t).start()
        return 0

    lax.fori_loop(1, n_dev, at_start, 0)
    atr[me] = ats[g]

    def at_wait(t, _):
        o = (me + t) % n_dev
        rcopy(ats.at[o // C], atr.at[o], at_s.at[t], at_r.at[o], {"gx": o // C, "yz": o % C}).wait_recv()
        return 0

    lax.fori_loop(1, n_dev, at_wait, 0)

    ZT = Z * T

    def o_source(o):
        hl, r = from_w(o, M)
        rel, line, u = r // ZT, (r // T) % Z, r % T
        s, d, b = u // R, (u % R) // NB, u % NB
        dev = line * PAIR + jnp.where(rel == 0, y, 1 - y)
        return (dev * C + d) * QB + hl * W + s * NB + b

    ordered = mm(pick(HL * M, n_dev * QB, o_source), atr[...].reshape(n_dev * QB, DH)).astype(BF)
    for n in range(HL):
        att[:, pl.ds(n * DH, DH)] = ordered[n * M:(n + 1) * M]
    pltpu.make_async_copy(wo_h, wo, w_sem.at[NC + 1 + NB]).wait()

    tile = 256
    def y_copy(k):
        return rcopy(ys.at[k], yr.at[k], y_s.at[k], y_r.at[k], {"gx": yp})

    for k in range(NC):
        def project_out(n, _):
            at = pl.multiple_of(n * tile, tile)
            part = mm(att[...], wo[:, pl.ds(k * fc + at, tile)])
            own[:, pl.ds(k * fc + at, tile)] = part[:ZT]
            ys[k, :, pl.ds(at, tile)] = part[ZT:].astype(BF)
            return 0

        lax.fori_loop(0, fc // tile, project_out, 0)
        y_copy(k).start()

    def z_copy(k, t):
        o = (z + t) % Z
        return rcopy(zs.at[k, o], zr.at[k, z], z_s.at[k, t], z_r.at[k, z], {"gx": o * PAIR + y})

    for k in range(NC):
        y_copy(k).wait_recv()
        cols = pl.ds(k * fc, fc)
        own[:, cols] += yr[k].astype(F32)

        for t in range(1, Z):
            o = (z + t) % Z
            r = pl.ds(pl.multiple_of(o * T, T), T)
            parts = [own[r, pl.ds(k * fc + p * half, half)] for p in range(2)]
            zs[k, o] = jnp.concatenate(parts, 0).astype(BF)
            z_copy(k, t).start()

    for k in range(NC):
        total = []
        r = pl.ds(pl.multiple_of(z * T, T), T)
        for p in range(2):
            total.append(own[r, pl.ds(k * fc + p * half, half)])
        total = jnp.concatenate(total, 0)
        for t in range(1, Z):
            o = (z + t) % Z
            rcopy(zs.at[k, o], zr.at[k, o], z_s.at[k, t], z_r.at[k, o], {"gx": yp}).wait_recv()
            total = total + zr[k, o].astype(F32)
        for p in range(2):
            cols = pl.ds(k * fc + p * half, half)
            res = (total[p * T:(p + 1) * T] + x32[:, cols]).astype(BF)
            for s in range(S):
                out[s, :, cols] = res[s * R:(s + 1) * R]

    for k in range(NC):
        ag(k, 0).wait_send()
        y_copy(k).wait_send()
        for t in range(1, Z):
            ag(k, t).wait_send()
            fw(k, t).wait_send()
            z_copy(k, t).wait_send()

    def q_sent(t, _):
        kv_copy(t).wait_send()
        q_copy(t).wait_send()
        return 0

    lax.fori_loop(1, G, q_sent, 0)

    def at_sent(t, _):
        at_copy(t).wait_send()
        return 0

    lax.fori_loop(1, n_dev, at_sent, 0)


def shards(tokens, norm_gain, query_weight, kv_weight, out_weight, cache, cache_lengths):
    S, R, F = tokens.shape
    G = lax.axis_size("gx")
    C = lax.axis_size("yz")
    NB, CACHE, two = cache.shape
    DH = two // 2
    HL = query_weight.shape[1] // DH
    KVC = kv_weight.shape[1]
    NC = 4
    T = S * R
    Z = G // PAIR
    M = G * T
    fc = F // NC
    half = fc // 2
    QB = up(HL * S * NB, 16)
    NDEV = G * C
    dims = (G, C, S, R, F, NB, HL, DH, KVC, CACHE, NC, QB)
    V = pltpu.VMEM
    dma = pltpu.SemaphoreType.DMA
    width = HL * DH + LANES
    scratch = [
        V((F, HL * DH), BF), V((F, KVC), BF), V((HL * DH, F), BF), V((NB, CACHE + TAIL, two), BF),
        V((T, F), F32), V((2, T, LANES), F32), V((2, T, LANES), F32),
        V((NC, G, 2 * T, half), BF), V((M, F), BF), V((M, width), F32), V((M, width), F32),
        V((G, QB, DH), BF), V((G, QB, DH), BF), V((G, 16, LANES), BF), V((G, 16, LANES), BF),
        V((G, QB, DH), BF), V((NDEV, QB, DH), BF), V((M, HL * DH), BF),
        V((Z * T, F), F32), V((NC, Z * T, fc), BF), V((NC, Z * T, fc), BF),
        V((NC, Z, 2 * T, half), BF), V((NC, Z, 2 * T, half), BF),
        dma((NC + 2 + NB,)), dma((2,)), dma((NC, Z)), dma((NC, Z)), dma((NC, G)), dma((2,)),
        dma((G,)), dma((G,)), dma((G,)), dma((G,)), dma((NDEV,)), dma((NDEV,)),
        dma((NC,)), dma((NC,)), dma((NC, Z)), dma((NC, Z)),
    ]
    vm = pl.BlockSpec(memory_space=pltpu.VMEM)
    hbm = pl.BlockSpec(memory_space=pl.ANY)
    return pl.pallas_call(
        functools.partial(kernel, dims),
        out_shape=jax.ShapeDtypeStruct(tokens.shape, BF),
        in_specs=[pl.BlockSpec(memory_space=pltpu.SMEM), vm, vm, hbm, hbm, hbm, hbm],
        out_specs=vm,
        scratch_shapes=scratch,
        compiler_params=pltpu.CompilerParams(
            collective_id=0, has_side_effects=True, vmem_limit_bytes=58 * 1024 * 1024
        ),
        name="layer",
    )(cache_lengths, tokens, norm_gain.reshape(1, F), query_weight, kv_weight, out_weight, cache)


def solution(mesh):
    in_specs = (
        P(None, ("ga", "gx"), "yz"),
        P("yz"),
        P("yz", "gx"),
        P("yz", "gx"),
        P("gx", "yz"),
        P(("ga", "gx", "yz"), None, None),
        P(("ga", "gx", "yz")),
    )
    out_specs = P(None, ("ga", "gx"), "yz")
    return jax.shard_map(shards, mesh=mesh, in_specs=in_specs, out_specs=out_specs, check_vma=False)
```

```python
import functools

import jax
import jax.numpy as jnp
from jax import lax
from jax.experimental import pallas as pl
from jax.experimental.pallas import tpu as pltpu
from jax.sharding import PartitionSpec as P

BF = jnp.bfloat16
F32 = jnp.float32
TAIL = 128
PAIR = 2
LANES = 128


def up(n, m):
    return -(-n // m) * m


def iotas(shape):
    return lax.broadcasted_iota(jnp.int32, shape, 0), lax.broadcasted_iota(jnp.int32, shape, 1)


def pick(rows, cols, source):
    o, i = iotas((rows, cols))
    return jnp.where(source(o) == i, 1.0, 0.0).astype(BF)


def mm(a, b):
    return jnp.dot(a, b, preferred_element_type=F32)


def kernel(
    dims,
    lens, tok, gain, wq_h, wkv_h, wo_h, cache_h,
    out,
    wq, wkv, wo, ext, x32, st, st_r, xg, xall, acc, acc_r,
    qs, qr, kvs, kvr, ats, atr, att, own, ys, yr, zs, zr,
    w_sem, st_sem, ag_s, fw_s, ag_r, ac_sem, q_s, q_r, kv_s, kv_r, at_s, at_r, y_s, y_r, z_s, z_r,
):
    G, C, S, R, F, NB, HL, DH, KVC, CACHE, NC, QB = dims
    T = S * R
    Z = G // PAIR
    H = G * HL
    M = G * T
    fc = F // NC
    half = fc // 2
    W = S * NB
    QW = HL * DH
    g = lax.axis_index("gx")
    c = lax.axis_index("yz")
    z = g // PAIR
    y = g % PAIR
    yp = z * PAIR + (1 - y)

    for k in range(NC):
        rows = pl.ds(k * fc, fc)
        pltpu.make_async_copy(wq_h.at[rows], wq.at[rows], w_sem.at[k]).start()
    pltpu.make_async_copy(wkv_h, wkv, w_sem.at[NC]).start()
    for b in range(NB):
        pltpu.make_async_copy(cache_h.at[b], ext.at[b, pl.ds(0, CACHE)], w_sem.at[NC + 1 + b]).start()
    pltpu.make_async_copy(wo_h, wo, w_sem.at[NC + 1 + NB]).start()

    bar = pltpu.get_barrier_semaphore()
    n_dev = G * C
    me = g * C + c

    def greet(t, _):
        o = (me + t) % n_dev
        pl.semaphore_signal(bar, inc=1, device_id={"gx": o // C, "yz": o % C}, device_id_type=pl.DeviceIdType.MESH)
        return 0

    lax.fori_loop(1, n_dev, greet, 0)

    for s in range(S):
        x32[pl.ds(s * R, R), :] = tok[s].astype(F32)
    x = x32[...]
    st[0] = jnp.broadcast_to(jnp.sum(x, -1, keepdims=True), (T, LANES))
    st[1] = jnp.broadcast_to(jnp.sum(x * x, -1, keepdims=True), (T, LANES))
    pl.semaphore_wait(bar, n_dev - 1)

    def rcopy(src, dst, ss, rs, dev):
        return pltpu.make_async_remote_copy(
            src_ref=src, dst_ref=dst, send_sem=ss, recv_sem=rs, device_id=dev, device_id_type=pl.DeviceIdType.MESH
        )

    st_copy = rcopy(st, st_r, st_sem.at[0], st_sem.at[1], {"yz": 1 - c})
    st_copy.start()
    for b in range(NB):
        ext[b, pl.ds(CACHE, TAIL), :] = jnp.zeros((TAIL, 2 * DH), BF)
    acc[...] = jnp.zeros_like(acc)
    st_copy.wait()
    D = F * C
    average = ((st[0] + st_r[0]) / D)[:, :1]
    spread = ((st[1] + st_r[1]) / D)[:, :1] - average * average
    inv = lax.rsqrt(spread + 1e-05)

    def ag(k, t):
        dev = yp if t == 0 else ((z + t) % Z) * PAIR + y
        return rcopy(xg.at[k, g], xg.at[k, g], ag_s.at[k, t], ag_r.at[k, g], {"gx": dev})

    def fw(k, t):
        o = ((z + t) % Z) * PAIR + y
        return rcopy(xg.at[k, o], xg.at[k, o], fw_s.at[k, t], ag_r.at[k, o], {"gx": yp})

    gains = gain[...].astype(F32)
    for k in range(NC):
        parts = []
        for p in range(2):
            cols = pl.ds(k * fc + p * half, half)
            first = (k * fc + p * half) // LANES
            row = jnp.concatenate([gains[first + i:first + i + 1] for i in range(half // LANES)], 1)
            parts.append((x32[:, cols] - average) * inv * row)
        xg[k, g] = jnp.concatenate(parts, 0).astype(BF)
        for t in range(1, Z):
            ag(k, t).start()
        ag(k, 0).start()

    for k in range(NC):
        for t in range(1, Z):
            o = ((z + t) % Z) * PAIR + y
            rcopy(xg.at[k, o], xg.at[k, o], fw_s.at[k, t], ag_r.at[k, o], {"gx": yp}).wait_recv()
            fw(k, t).start()

    for k in range(NC):
        for t in range(Z):
            o = ((z + t) % Z) * PAIR + (1 - y)
            rcopy(xg.at[k, o], xg.at[k, o], fw_s.at[k, t], ag_r.at[k, o], {"gx": yp}).wait_recv()
        rows = pl.ds(k * fc, fc)
        for p in range(2):
            block = xg[k].astype(F32)[:, p * T:(p + 1) * T, :].reshape(M, half)
            xall[:, pl.ds(k * fc + p * half, half)] = block.astype(BF)
        pltpu.make_async_copy(wq_h.at[rows], wq.at[rows], w_sem.at[k]).wait()
        if k == 0:
            pltpu.make_async_copy(wkv_h, wkv, w_sem.at[NC]).wait()

        def project(n, _):
            cols = pl.ds(pl.multiple_of(n * DH, DH), DH)
            acc[:, cols] += mm(xall[:, rows], wq[rows, cols])
            return 0

        lax.fori_loop(0, HL, project, 0)
        acc[:, pl.ds(QW, KVC)] += lax.dot_general(
            xall[:, rows], wkv[:, rows], (((1,), (1,)), ((), ())), preferred_element_type=F32
        )

    ac = rcopy(acc, acc_r, ac_sem.at[0], ac_sem.at[1], {"yz": 1 - c})
    ac.start()
    ac.wait()

    def from_w(o, width):
        return o // width, o % width

    def q_source(o):
        d, w = from_w(o, QB)
        hl, s, b = w // W, (w // NB) % S, w % NB
        return jnp.where(w < HL * W, hl * M + d * T + s * R + c * NB + b, -1)

    def kv_source(o):
        d, w = from_w(o, 16)
        return jnp.where(w < W, d * T + (w // NB) * R + c * NB + w % NB, -1)

    kv_all = (acc[:, pl.ds(QW, LANES)] + acc_r[:, pl.ds(QW, LANES)]).astype(BF)
    kvs[...] = mm(pick(G * 16, M, kv_source), kv_all).astype(BF).reshape(G, 16, LANES)
    q_all = jnp.concatenate(
        [(acc[:, pl.ds(n * DH, DH)] + acc_r[:, pl.ds(n * DH, DH)]).astype(BF) for n in range(HL)], 0
    )
    qs[...] = mm(pick(G * QB, HL * M, q_source), q_all).astype(BF).reshape(G, QB, DH)

    def q_copy(t):
        o = (g + t) % G
        return rcopy(qs.at[o], qr.at[g], q_s.at[t], q_r.at[g], {"gx": o})

    def kv_copy(t):
        o = (g + t) % G
        return rcopy(kvs.at[o], kvr.at[g], kv_s.at[t], kv_r.at[g], {"gx": o})

    def q_start(t, _):
        kv_copy(t).start()
        q_copy(t).start()
        return 0

    lax.fori_loop(1, G, q_start, 0)
    kvr[g] = kvs[g]
    qr[g] = qs[g]

    def q_wait(t, _):
        o = (g + t) % G
        rcopy(kvs.at[o], kvr.at[o], kv_s.at[t], kv_r.at[o], {"gx": o}).wait_recv()
        rcopy(qs.at[o], qr.at[o], q_s.at[t], q_r.at[o], {"gx": o}).wait_recv()
        return 0

    lax.fori_loop(1, G, q_wait, 0)

    fresh = jnp.zeros((16, 2 * DH), F32)
    for d in range(G):
        i, n = iotas((LANES, 2 * DH))
        spread_cols = jnp.where((i < KVC) & (n == i + d * KVC), 1.0, 0.0).astype(BF)
        fresh = fresh + mm(kvr[d], spread_cols)
    fresh = fresh.astype(BF)
    for b in range(NB):
        rows_b = mm(pick(16, 16, lambda o: jnp.where(o < S, o * NB + b, -1)), fresh)
        ext[b, pl.ds(CACHE, 16), :] = rows_b.astype(BF)

    HS = H * S

    def r_source(o):
        b, h, s = o // HS, (o // S) % H, o % S
        return (h // HL) * QB + (h % HL) * W + s * NB + b

    query = mm(pick(NB * HS, G * QB, r_source), qr[...].reshape(G * QB, DH)).astype(BF)
    slots = CACHE + TAIL
    factor = DH ** (-0.5)
    outs = []
    for b in range(NB):
        pltpu.make_async_copy(cache_h.at[b], ext.at[b, pl.ds(0, CACHE)], w_sem.at[NC + 1 + b]).wait()
        qb = query[b * HS:(b + 1) * HS]
        scores = lax.dot_general(
            qb, ext[b, :, pl.ds(0, DH)], (((1,), (1,)), ((), ())), preferred_element_type=F32
        ) * factor
        row, slot = iotas((HS, slots))
        seen = (slot < lens[b]) | ((slot >= CACHE) & (slot - CACHE <= row % S))
        scores = jnp.where(seen, scores, -jnp.inf)
        raised = jnp.exp(scores - jnp.max(scores, -1, keepdims=True))
        weights = (raised / jnp.sum(raised, -1, keepdims=True)).astype(BF)
        outs.append(mm(weights, ext[b, :, pl.ds(DH, DH)]).astype(BF))
    attended = jnp.concatenate(outs, 0)

    def a_source(o):
        d, w = from_w(o, QB)
        hl, s, b = w // W, (w // NB) % S, w % NB
        return jnp.where(w < HL * W, b * HS + (d * HL + hl) * S + s, -1)

    ats[...] = mm(pick(G * QB, NB * HS, a_source), attended).astype(BF).reshape(G, QB, DH)

    def at_copy(t):
        o = (me + t) % n_dev
        return rcopy(ats.at[o // C], atr.at[me], at_s.at[t], at_r.at[me], {"gx": o // C, "yz": o % C})

    def at_start(t, _):
        at_copy(t).start()
        return 0

    lax.fori_loop(1, n_dev, at_start, 0)
    atr[me] = ats[g]

    def at_wait(t, _):
        o = (me + t) % n_dev
        rcopy(ats.at[o // C], atr.at[o], at_s.at[t], at_r.at[o], {"gx": o // C, "yz": o % C}).wait_recv()
        return 0

    lax.fori_loop(1, n_dev, at_wait, 0)

    ZT = Z * T

    def o_source(o):
        hl, r = from_w(o, M)
        rel, line, u = r // ZT, (r // T) % Z, r % T
        s, d, b = u // R, (u % R) // NB, u % NB
        dev = line * PAIR + jnp.where(rel == 0, y, 1 - y)
        return (dev * C + d) * QB + hl * W + s * NB + b

    ordered = mm(pick(HL * M, n_dev * QB, o_source), atr[...].reshape(n_dev * QB, DH)).astype(BF)
    for n in range(HL):
        att[:, pl.ds(n * DH, DH)] = ordered[n * M:(n + 1) * M]
    pltpu.make_async_copy(wo_h, wo, w_sem.at[NC + 1 + NB]).wait()

    tile = 256
    def y_copy(k):
        return rcopy(ys.at[k], yr.at[k], y_s.at[k], y_r.at[k], {"gx": yp})

    for k in range(NC):
        def project_out(n, _):
            at = pl.multiple_of(n * tile, tile)
            part = mm(att[...], wo[:, pl.ds(k * fc + at, tile)])
            own[:, pl.ds(k * fc + at, tile)] = part[:ZT]
            ys[k, :, pl.ds(at, tile)] = part[ZT:].astype(BF)
            return 0

        lax.fori_loop(0, fc // tile, project_out, 0)
        y_copy(k).start()

    def z_copy(k, t):
        o = (z + t) % Z
        return rcopy(zs.at[k, o], zr.at[k, z], z_s.at[k, t], z_r.at[k, z], {"gx": o * PAIR + y})

    for k in range(NC):
        y_copy(k).wait_recv()
        cols = pl.ds(k * fc, fc)
        own[:, cols] += yr[k].astype(F32)

        for t in range(1, Z):
            o = (z + t) % Z
            r = pl.ds(pl.multiple_of(o * T, T), T)
            parts = [own[r, pl.ds(k * fc + p * half, half)] for p in range(2)]
            zs[k, o] = jnp.concatenate(parts, 0).astype(BF)
            z_copy(k, t).start()

    for k in range(NC):
        total = []
        r = pl.ds(pl.multiple_of(z * T, T), T)
        for p in range(2):
            total.append(own[r, pl.ds(k * fc + p * half, half)])
        total = jnp.concatenate(total, 0)
        for t in range(1, Z):
            o = (z + t) % Z
            rcopy(zs.at[k, o], zr.at[k, o], z_s.at[k, t], z_r.at[k, o], {"gx": yp}).wait_recv()
            total = total + zr[k, o].astype(F32)
        for p in range(2):
            cols = pl.ds(k * fc + p * half, half)
            res = (total[p * T:(p + 1) * T] + x32[:, cols]).astype(BF)
            for s in range(S):
                out[s, :, cols] = res[s * R:(s + 1) * R]

    for k in range(NC):
        ag(k, 0).wait_send()
        y_copy(k).wait_send()
        for t in range(1, Z):
            ag(k, t).wait_send()
            fw(k, t).wait_send()
            z_copy(k, t).wait_send()

    def q_sent(t, _):
        kv_copy(t).wait_send()
        q_copy(t).wait_send()
        return 0

    lax.fori_loop(1, G, q_sent, 0)

    def at_sent(t, _):
        at_copy(t).wait_send()
        return 0

    lax.fori_loop(1, n_dev, at_sent, 0)


def shards(tokens, norm_gain, query_weight, kv_weight, out_weight, cache, cache_lengths):
    S, R, F = tokens.shape
    G = lax.axis_size("gx")
    C = lax.axis_size("yz")
    NB, CACHE, two = cache.shape
    DH = two // 2
    HL = query_weight.shape[1] // DH
    KVC = kv_weight.shape[1]
    NC = 4
    T = S * R
    Z = G // PAIR
    M = G * T
    fc = F // NC
    half = fc // 2
    QB = up(HL * S * NB, 16)
    NDEV = G * C
    dims = (G, C, S, R, F, NB, HL, DH, KVC, CACHE, NC, QB)
    V = pltpu.VMEM
    dma = pltpu.SemaphoreType.DMA
    width = HL * DH + LANES
    scratch = [
        V((F, HL * DH), BF), V((KVC, F), BF), V((HL * DH, F), BF), V((NB, CACHE + TAIL, two), BF),
        V((T, F), F32), V((2, T, LANES), F32), V((2, T, LANES), F32),
        V((NC, G, 2 * T, half), BF), V((M, F), BF), V((M, width), F32), V((M, width), F32),
        V((G, QB, DH), BF), V((G, QB, DH), BF), V((G, 16, LANES), BF), V((G, 16, LANES), BF),
        V((G, QB, DH), BF), V((NDEV, QB, DH), BF), V((M, HL * DH), BF),
        V((Z * T, F), F32), V((NC, Z * T, fc), BF), V((NC, Z * T, fc), BF),
        V((NC, Z, 2 * T, half), BF), V((NC, Z, 2 * T, half), BF),
        dma((NC + 2 + NB,)), dma((2,)), dma((NC, Z)), dma((NC, Z)), dma((NC, G)), dma((2,)),
        dma((G,)), dma((G,)), dma((G,)), dma((G,)), dma((NDEV,)), dma((NDEV,)),
        dma((NC,)), dma((NC,)), dma((NC, Z)), dma((NC, Z)),
    ]
    vm = pl.BlockSpec(memory_space=pltpu.VMEM)
    hbm = pl.BlockSpec(memory_space=pl.ANY)
    return pl.pallas_call(
        functools.partial(kernel, dims),
        out_shape=jax.ShapeDtypeStruct(tokens.shape, BF),
        in_specs=[pl.BlockSpec(memory_space=pltpu.SMEM), vm, vm, hbm, hbm, hbm, hbm],
        out_specs=vm,
        scratch_shapes=scratch,
        compiler_params=pltpu.CompilerParams(
            collective_id=0, has_side_effects=True, vmem_limit_bytes=58 * 1024 * 1024
        ),
        name="layer",
    )(cache_lengths, tokens, norm_gain.reshape(F // LANES, LANES), query_weight, kv_weight.T, out_weight, cache)


def solution(mesh):
    in_specs = (
        P(None, ("ga", "gx"), "yz"),
        P("yz"),
        P("yz", "gx"),
        P("yz", "gx"),
        P("gx", "yz"),
        P(("ga", "gx", "yz"), None, None),
        P(("ga", "gx", "yz")),
    )
    out_specs = P(None, ("ga", "gx"), "yz")
    return jax.shard_map(shards, mesh=mesh, in_specs=in_specs, out_specs=out_specs, check_vma=False)
```
